512 devices in a mesh: dp: 16 (over y, z_hi, core), fsdp: 32 (over x, z_lo).
Axes of the slice: x: 4, y: 4, z: 16 (z_hi: 2, z_lo: 8; z = z_hi * 8 + z_lo), core: 2. Of those that a mesh axis runs over, the one named last changes fastest.
Arguments:
- activations: bfloat16 [1024, 8192], P('fsdp', 'dp'), may hold values from -6 to 6
- cotangents: bfloat16 [1024, 8192], P('fsdp', 'dp'), may hold values from -6 to 6
- gate_weight: bfloat16 [8192, 14336], P('dp', 'fsdp'), may hold values from -0.0625 to 0.0625
- down_weight: bfloat16 [14336, 8192], P('fsdp', 'dp'), may hold values from -0.046875 to 0.046875
- query_grads: bfloat16 [8, 8192, 14336], P(None, 'dp', 'fsdp'), may hold values from -0.0012207031 to 0.0012207031
Outputs:
- scores: float32 [1024, 8], P(('dp', 'fsdp'))
The draws below stay inside these ranges and needn't reach their ends.
All inputs are finite; a program needn't handle non-finite values.
Results may differ from the reference program's by a relative error of at most 0.0075.
Values may be sent and summed in bfloat16 or wider, within the bound.
A program may use at most 64 MiB of HBM per device.

```python
import jax
import jax.numpy as jnp
from jax import lax

D = 8192
FF = 14336
NQ = 8
TOKENS = 1024


def levels(rng, extent, split, least, top_value):
    factor_of = 1.0
    for axis_at, shards_of in split:
        steps = jax.random.uniform(jax.random.fold_in(jax.random.fold_in(rng, 6), axis_at), (shards_of,), jnp.float32, least / len(split), top_value / len(split))
        factor_of = factor_of * jnp.repeat(jnp.exp(steps), extent[axis_at] // shards_of).reshape((-1,) + (1,) * (len(extent) - 1 - axis_at))
    return factor_of


def centred(rng, dims, spread, reach, shards=(), kind=jnp.bfloat16):
    array = jax.random.normal(rng, dims, jnp.float32) * spread
    if len(shards) > 0:
        array = levels(rng, dims, shards, -0.22, 0.18) * array
    return jnp.clip(array, min=-reach, max=reach).astype(kind)


def setup_inputs(seed: int = 0) -> dict:
    key_list = jax.random.split(jax.random.key(seed), 6)
    return {
        "activations": centred(key_list[0], (TOKENS, D), 1.0, 6.0, ((0, 32), (1, 16))),
        "cotangents": centred(key_list[1], (TOKENS, D), 1.0, 6.0, ((0, 32), (1, 16))),
        "gate_weight": centred(key_list[2], (D, FF), D ** -0.5, 0.0625, ((0, 16), (1, 32))),
        "down_weight": centred(key_list[3], (FF, D), FF ** -0.5, 0.046875, ((0, 32), (1, 16))),
        "query_grads": centred(key_list[4], (NQ, D, FF), (D * FF // 5) ** -0.5, 0.0012207031, ((1, 16), (2, 32))),
    }


def reference(activations, cotangents, gate_weight, down_weight, query_grads):
    gate_sum = jnp.dot(activations, gate_weight, preferred_element_type=jnp.float32)
    back_sum = lax.dot_general(cotangents, down_weight, (((1,), (1,)), ((), ())), preferred_element_type=jnp.float32)
    signal = (jax.nn.silu(gate_sum) * back_sum).astype(jnp.bfloat16)
    signal_wide = signal.astype(jnp.float32)

    def one_query(query_grad):
        projected = jnp.dot(activations, query_grad, preferred_element_type=jnp.float32)
        return jnp.sum(projected * signal_wide, axis=1)

    per_query = lax.map(one_query, query_grads)
    return jnp.transpose(per_query)
```

```python
import functools

import jax
import jax.numpy as jnp
from jax import lax
from jax.experimental import pallas as pl
from jax.experimental.pallas import tpu as pltpu
from jax.sharding import PartitionSpec as P

MESH = pl.DeviceIdType.MESH
F32 = jnp.float32
BF16 = jnp.bfloat16
NY, NH, NC, NX, NZ = 4, 2, 2, 4, 8
CHUNKS = 4
WHOLE_H = (False, False, False, True)


def nearest(z, i):
    reach = jnp.minimum(z, NZ - 1 - z)
    inner = z - (i + 1) // 2 if i % 2 else z + i // 2
    outer = jnp.where(z < NZ // 2, i, NZ - 1 - i)
    return jnp.where(i <= 2 * reach, inner, outer)


def kernel(
    act, cot, gate_w, down_w, query, out,
    ag, gw, dw, qt, qg, actt,
    c_out, c_in, acc, y_out, y_in, acc2, h_out, h_in, sig,
    scores, f1_in, f1_acc, f2_in, f2_acc, f3_in,
    load, z_s, z_r, x_s, x_r, w_s, w_r,
    c_s, c_r, y_s, y_r, h_s, h_r, hs_s, hs_r, ys_s, ys_r, cs_s, cs_r,
    f1_s, f1_r, f2_s, f2_r, f3_s, f3_r,
):
    p, f = lax.axis_index("dp"), lax.axis_index("fsdp")
    y, h, c = p // 4, (p // 2) % 2, p % 2
    x, z = f // NZ, f % NZ

    def dev(dy=0, dh=0, dc=0, dx=0, dz=0):
        ty, th, tc = (y + dy) % NY, (h + dh) % NH, (c + dc) % NC
        tx, tz = (x + dx) % NX, z + dz
        return (ty * 4 + th * 2 + tc, tx * NZ + tz)

    rows, width = act.shape
    slab = NX * rows
    part, half = slab // NY, slab // NY // NH
    queries = query.shape[0]

    mine = pl.ds(pl.multiple_of(x * rows, rows), rows)
    loads = [
        pltpu.make_async_copy(act, ag.at[0, z, mine], load.at[0]),
        pltpu.make_async_copy(cot, ag.at[1, z, mine], load.at[1]),
        pltpu.make_async_copy(gate_w, gw, load.at[2]),
        pltpu.make_async_copy(down_w, dw, load.at[3]),
        pltpu.make_async_copy(query, qt, load.at[4]),
    ]
    for item in loads:
        item.start()

    barrier = pltpu.get_barrier_semaphore()

    def greet(device):
        pl.semaphore_signal(barrier, inc=1, device_id=device, device_id_type=MESH)

    greet(dev(dx=1))
    greet(dev(dx=3))
    pl.when(z > 0)(lambda: greet(dev(dz=-1)))
    pl.when(z < NZ - 1)(lambda: greet(dev(dz=1)))
    greet(dev(dc=1))
    for dy in range(1, NY):
        greet(dev(dy=dy))
    greet(dev(dh=1))
    loads[0].wait()
    loads[1].wait()
    line = jnp.where(z > 0, 1, 0) + jnp.where(z < NZ - 1, 1, 0)
    pl.semaphore_wait(barrier, line + 7)

    def remote(src, dst, send, recv, device):
        return pltpu.make_async_remote_copy(
            src_ref=src, dst_ref=dst, send_sem=send, recv_sem=recv,
            device_id=device, device_id_type=MESH,
        )

    sides = [(s, d) for s in range(NZ) for d in range(2) if s or not d]

    def valid(s, d):
        return z >= s if d == 0 else z + s <= NZ - 1

    def at_z(s, d):
        return jnp.clip(z - s if d == 0 else z + s, 0, NZ - 1)

    def spot(zz, xx):
        return (zz, pl.ds(pl.multiple_of(xx * rows, rows), rows))

    def z_copy(s, d):
        where = spot(at_z(s - 1, d), x)
        block = ag.at[:, where[0], where[1]]
        return remote(block, block, z_s.at[d, s], z_r.at[d, s], dev(dz=1 - 2 * d))

    def z_land(s, d):
        where = spot(at_z(s, d), x)
        block = ag.at[:, where[0], where[1]]
        return remote(block, block, z_s.at[d, s], z_r.at[d, s], dev(dz=2 * d - 1))

    def x_copy(s, d, e):
        where = spot(at_z(s, d), x)
        block = ag.at[:, where[0], where[1]]
        k = 2 * s + d
        return remote(block, block, x_s.at[e, k], x_r.at[e, k], dev(dx=1 + 2 * e))

    def x_land(s, d, e):
        where = spot(at_z(s, d), (x + 3 - 2 * e) % NX)
        block = ag.at[:, where[0], where[1]]
        k = 2 * s + d
        return remote(block, block, x_s.at[e, k], x_r.at[e, k], dev(dx=3 - 2 * e))

    def w_copy(s, d, e):
        where = spot(at_z(s, d), (x + 3 - 2 * e) % NX)
        block = ag.at[e, where[0], where[1]]
        k = 2 * s + d
        return remote(block, block, w_s.at[e, k], w_r.at[e, k], dev(dx=1 + 2 * e))

    def w_land(s, d, e):
        where = spot(at_z(s, d), (x + 2) % NX)
        block = ag.at[e, where[0], where[1]]
        k = 2 * s + d
        return remote(block, block, w_s.at[e, k], w_r.at[e, k], dev(dx=3 - 2 * e))

    def ds_of(s):
        return (0,) if s == 0 else (0, 1)

    def step_z(s):
        for d in ds_of(s):
            def body(d=d):
                if s:
                    z_land(s, d).wait_recv()
                if s < NZ - 1:
                    if s:
                        pl.when(z < NZ - 1 if d == 0 else z > 0)(lambda: z_copy(s + 1, d).start())
                    else:
                        pl.when(z < NZ - 1)(lambda: z_copy(1, 0).start())
                        pl.when(z > 0)(lambda: z_copy(1, 1).start())
                x_copy(s, d, 0).start()
                x_copy(s, d, 1).start()
            pl.when(valid(s, d))(body)

    def step_x(s):
        for d in ds_of(s):
            def body(d=d):
                for e in range(2):
                    x_land(s, d, e).wait_recv()
                    w_copy(s, d, e).start()
            pl.when(valid(s, d))(body)

    def step_w(s):
        for d in ds_of(s):
            def body(d=d):
                for e in range(2):
                    w_land(s, d, e).wait_recv()
            pl.when(valid(s, d))(body)

    def drain_gather():
        for s, d in sides:
            if s:
                going = (z >= s - 1) & (z < NZ - 1) if d == 0 else (z + s - 1 <= NZ - 1) & (z > 0)
                pl.when(going)(lambda s=s, d=d: z_copy(s, d).wait_send())

            def body(s=s, d=d):
                for e in range(2):
                    x_copy(s, d, e).wait_send()
                    w_copy(s, d, e).wait_send()
            pl.when(valid(s, d))(body)

    def turn_queries(first, count):
        def one(q, carry):
            qg[q] = qt[q].T
            return carry

        lax.fori_loop(first, first + count, one, 0)

    def products(zz, store):
        for n, weight in enumerate((gw, dw)):
            store(n, lax.dot_general(
                ag[n, zz], weight[...], (((1,), (1,)), ((), ())), preferred_element_type=F32
            ))

    def slab_of(k, core):
        first, second = nearest(z, 2 * k), nearest(z, 2 * k + 1)
        return jnp.where(core == 0, first, second)

    def c_copy(k):
        return remote(c_out.at[k], c_in.at[k], c_s.at[k], c_r.at[k], dev(dc=1))

    def stage_products(k):
        def to_peer(n, value):
            c_out[k, n] = value.astype(BF16)

        def to_own(n, value):
            acc[k, n] = value

        products(slab_of(k, 1 - c), to_peer)
        c_copy(k).start()
        products(slab_of(k, c), to_own)

    def y_rows(yy):
        return pl.ds(pl.multiple_of(yy * part, part), part)

    def y_copy(k, dy):
        return remote(
            y_out.at[k, :, y_rows((y + dy) % NY)], y_in.at[k, dy - 1],
            y_s.at[k, dy - 1], y_r.at[k, dy - 1], dev(dy=dy),
        )

    def stage_core(k):
        c_copy(k).wait_recv()
        total = acc[k] + c_in[k].astype(F32)
        acc[k] = total
        y_out[k] = total.astype(BF16)
        for dy in (2, 1, 3):
            y_copy(k, dy).start()

    def h_rows(hh):
        return pl.ds(pl.multiple_of(hh * half, half), half)

    def h_copy(k):
        if WHOLE_H[k]:
            return remote(h_out.at[k], h_in.at[k], h_s.at[k], h_r.at[k], dev(dh=1))
        return remote(
            h_out.at[k, :, h_rows(1 - h)], h_in.at[k, :, pl.ds(0, half)],
            h_s.at[k], h_r.at[k], dev(dh=1),
        )

    def stage_y(k):
        total = acc[k, :, y_rows(y)]
        for dy in range(1, NY):
            y_copy(k, dy).wait_recv()
            total = total + y_in[k, dy - 1].astype(F32)
        acc2[k] = total
        h_out[k] = total.astype(BF16)
        h_copy(k).start()

    def s_rows(yy, hh):
        return pl.ds(pl.multiple_of(yy * part + hh * half, half), half)

    def hs_copy(k):
        block = sig.at[k, c, s_rows(y, h)]
        return remote(block, block, hs_s.at[k], hs_r.at[k], dev(dh=1))

    def hs_land(k):
        block = sig.at[k, c, s_rows(y, 1 - h)]
        return remote(block, block, hs_s.at[k], hs_r.at[k], dev(dh=1))

    def ys_copy(k, dy):
        block = sig.at[k, c, y_rows(y)]
        return remote(block, block, ys_s.at[k, dy - 1], ys_r.at[k, dy - 1], dev(dy=dy))

    def ys_land(k, dy):
        block = sig.at[k, c, y_rows((y + NY - dy) % NY)]
        return remote(block, block, ys_s.at[k, dy - 1], ys_r.at[k, dy - 1], dev(dy=dy))

    def cs_copy(k):
        block = sig.at[k, c]
        return remote(block, block, cs_s.at[k], cs_r.at[k], dev(dc=1))

    def cs_land(k):
        block = sig.at[k, 1 - c]
        return remote(block, block, cs_s.at[k], cs_r.at[k], dev(dc=1))

    def signal_of(total):
        gate, back = total[0], total[1]
        return (gate / (1.0 + jnp.exp(-gate)) * back).astype(BF16)

    def stage_h(k):
        h_copy(k).wait_recv()
        if WHOLE_H[k]:
            sig[k, c, y_rows(y)] = signal_of(acc2[k] + h_in[k].astype(F32))
            for dy in (2, 1, 3):
                ys_copy(k, dy).start()
        else:
            total = acc2[k, :, h_rows(h)] + h_in[k, :, pl.ds(0, half)].astype(F32)
            sig[k, c, s_rows(y, h)] = signal_of(total)
            hs_copy(k).start()

    def stage_hs(k):
        if not WHOLE_H[k]:
            hs_land(k).wait_recv()
            for dy in (2, 1, 3):
                ys_copy(k, dy).start()

    def stage_ys(k):
        for dy in range(1, NY):
            ys_land(k, dy).wait_recv()
        cs_copy(k).start()

    def turn(k):
        for n in range(2):
            actt[k, :, n * slab:(n + 1) * slab] = ag[0, nearest(z, 2 * k + n)].astype(F32).T

    def stage_scores(k):
        cs_land(k).wait_recv()
        both = sig[k].reshape(2 * slab, sig.shape[-1])
        first, second = nearest(z, 2 * k), nearest(z, 2 * k + 1)

        def one(q, carry):
            back = lax.dot_general(
                qg[q], both, (((1,), (1,)), ((), ())), preferred_element_type=F32
            )
            line = jnp.sum(back * actt[k], axis=0, keepdims=True)
            scores[first, pl.ds(q, 1), :] = line[:, :slab]
            scores[second, pl.ds(q, 1), :] = line[:, slab:]
            return carry

        lax.fori_loop(0, queries, one, 0)

    def drain_chunk(k):
        c_copy(k).wait_send()
        h_copy(k).wait_send()
        if not WHOLE_H[k]:
            hs_copy(k).wait_send()
        for dy in range(1, NY):
            y_copy(k, dy).wait_send()
            ys_copy(k, dy).wait_send()
        cs_copy(k).wait_send()

    for step in range(NZ + 2):
        if step < NZ:
            step_z(step)
        if 1 <= step < NZ + 1:
            step_x(step - 1)
        if step >= 2:
            step_w(step - 2)
        if step == 0:
            loads[4].wait()
        if step < 4:
            turn_queries(2 * step, 2)
        if step == 2:
            loads[2].wait()
            loads[3].wait()
        ready = step - 2
        if ready >= 1 and ready % 2 == 1:
            k = ready // 2
            stage_products(k)
            turn(k)
        if ready >= 1:
            k = (ready - 1) // 2
            if ready % 2 == 0:
                stage_core(k)
            elif k >= 1:
                stage_y(k - 1)
    last = CHUNKS - 1
    stage_core(last)
    stage_h(0)
    stage_h(1)
    stage_y(last)
    stage_hs(0)
    stage_h(2)
    stage_hs(1)
    stage_ys(0)
    stage_ys(1)
    stage_scores(0)
    stage_hs(2)
    stage_scores(1)
    stage_h(last)
    stage_ys(2)
    stage_scores(2)
    stage_ys(last)
    stage_scores(last)

    def by_dest(core):
        return [(hh, xh, 4 * hh + 2 * core + xh) for hh in range(2) for xh in range(2)]

    f1_copies = [
        remote(
            scores.at[pl.ds(pl.multiple_of(4 * hh + 2 * (1 - c), 2), 2)], f1_in.at[hh],
            f1_s.at[hh], f1_r.at[hh], dev(dc=1),
        )
        for hh in range(2)
    ]
    for item in f1_copies:
        item.start()
    for item in f1_copies:
        item.wait_recv()
    for hh, xh, tile in by_dest(c):
        f1_acc[xh, hh] = scores[tile] + f1_in[hh, xh]

    f2_copies = []
    for dx in range(NX):
        for dy in range(NY):
            if dx or dy:
                n = dx * NY + dy - 1
                f2_copies.append(
                    remote(
                        f1_acc.at[((x + dx) % NX) // 2], f2_in.at[n],
                        f2_s.at[n], f2_r.at[n], dev(dx=dx, dy=dy),
                    )
                )
    for item in f2_copies:
        item.start()
    total = f1_acc[x // 2]
    for n, item in enumerate(f2_copies):
        item.wait_recv()
        total = total + f2_in[n]
    f2_acc[...] = total

    f3_copies = []
    for dh in range(NH):
        for dz in range(NZ):
            if dh or dz:
                n = dh * NZ + dz - 1
                tz = (z + dz) % NZ
                f3_copies.append(
                    remote(
                        f2_acc.at[(h + dh) % NH], f3_in.at[n],
                        f3_s.at[n], f3_r.at[n], dev(dh=dh, dz=tz - z),
                    )
                )
    for item in reversed(f3_copies):
        item.start()
    total = f2_acc[h]
    for n, item in enumerate(f3_copies):
        item.wait_recv()
        total = total + f3_in[n]
    lane = y * 32 + (x % 2) * 16 + z * 2
    moved = pltpu.roll(total, (slab - lane) % slab, 1)
    out[...] = moved.T[0:2, :]

    drain_gather()
    for k in range(CHUNKS):
        drain_chunk(k)
    for item in f1_copies + f2_copies + f3_copies:
        item.wait_send()


def per_device(activations, cotangents, gate_weight, down_weight, query_grads):
    rows, width = activations.shape
    hidden = gate_weight.shape[1]
    queries = query_grads.shape[0]
    slab = NX * rows
    part = slab // NY
    dma, vmem = pltpu.SemaphoreType.DMA, pltpu.VMEM
    n = CHUNKS
    scratch = [
        vmem((2, NZ, slab, width), BF16),
        vmem((hidden, width), BF16),
        vmem((hidden, width), BF16),
        vmem((queries, hidden, width), BF16),
        vmem((queries, width, hidden), BF16),
        vmem((n, width, 2 * slab), F32),
        vmem((n, 2, slab, hidden), BF16),
        vmem((n, 2, slab, hidden), BF16),
        vmem((n, 2, slab, hidden), F32),
        vmem((n, 2, slab, hidden), BF16),
        vmem((n, NY - 1, 2, part, hidden), BF16),
        vmem((n, 2, part, hidden), F32),
        vmem((n, 2, part, hidden), BF16),
        vmem((n, 2, part, hidden), BF16),
        vmem((n, 2, slab, hidden), BF16),
        vmem((NZ, queries, slab), F32),
        vmem((2, 2, queries, slab), F32),
        vmem((2, 2, queries, slab), F32),
        vmem((NX * NY - 1, 2, queries, slab), F32),
        vmem((2, queries, slab), F32),
        vmem((NH * NZ - 1, queries, slab), F32),
        dma((5,)),
        dma((2, NZ)), dma((2, NZ)),
        dma((2, 2 * NZ)), dma((2, 2 * NZ)),
        dma((2, 2 * NZ)), dma((2, 2 * NZ)),
        dma((n,)), dma((n,)),
        dma((n, NY - 1)), dma((n, NY - 1)),
        dma((n,)), dma((n,)),
        dma((n,)), dma((n,)),
        dma((n, NY - 1)), dma((n, NY - 1)),
        dma((n,)), dma((n,)),
        dma((2,)), dma((2,)),
        dma((NX * NY - 1,)), dma((NX * NY - 1,)),
        dma((NH * NZ - 1,)), dma((NH * NZ - 1,)),
    ]
    return pl.pallas_call(
        kernel,
        name="influence_scores",
        out_shape=jax.ShapeDtypeStruct((2, queries), F32),
        in_specs=[pl.BlockSpec(memory_space=pl.ANY)] * 5,
        out_specs=pl.BlockSpec(memory_space=pltpu.VMEM),
        scratch_shapes=scratch,
        cost_estimate=pl.CostEstimate(
            flops=2 * NZ * slab * width * hidden * (2 + queries),
            bytes_accessed=2 * width * hidden * (2 + queries),
            transcendentals=2 * part * hidden,
        ),
        compiler_params=pltpu.CompilerParams(
            collective_id=0, has_side_effects=True, vmem_limit_bytes=56 * 2**20
        ),
    )(activations, cotangents, gate_weight.T, down_weight, jnp.swapaxes(query_grads, 1, 2))


def solution(mesh):
    placed = (
        P("fsdp", "dp"),
        P("fsdp", "dp"),
        P("dp", "fsdp"),
        P("fsdp", "dp"),
        P(None, "dp", "fsdp"),
    )
    return jax.shard_map(
        per_device, mesh=mesh, in_specs=placed, out_specs=P(("dp", "fsdp"), None), check_vma=False
    )
```

```python
import functools

import jax
import jax.numpy as jnp
from jax import lax
from jax.experimental import pallas as pl
from jax.experimental.pallas import tpu as pltpu
from jax.sharding import PartitionSpec as P

MESH = pl.DeviceIdType.MESH
F32 = jnp.float32
BF16 = jnp.bfloat16
NY, NH, NC, NX, NZ = 4, 2, 2, 4, 8
REACH = 1
CHUNKS = 4
WHOLE_H = (False, False, False, True)


def nearest(z, i):
    reach = jnp.minimum(z, NZ - 1 - z)
    inner = z - (i + 1) // 2 if i % 2 else z + i // 2
    outer = jnp.where(z < NZ // 2, i, NZ - 1 - i)
    return jnp.where(i <= 2 * reach, inner, outer)


def kernel(
    act, cot, gate_w, down_w, query, out,
    ag, gw, dw, qt, qg, actt,
    c_out, c_in, acc, y_out, y_in, acc2, h_out, h_in, sig,
    scores, f1_in, f1_acc, f2_in, f2_acc, f3_in,
    told, load, z_s, z_r, x_s, x_r, w_s, w_r,
    c_s, c_r, y_s, y_r, h_s, h_r, hs_s, hs_r, ys_s, ys_r, cs_s, cs_r,
    f1_s, f1_r, f2_s, f2_r, f3_s, f3_r,
):
    p, f = lax.axis_index("dp"), lax.axis_index("fsdp")
    y, h, c = p // 4, (p // 2) % 2, p % 2
    x, z = f // NZ, f % NZ

    def dev(dy=0, dh=0, dc=0, dx=0, dz=0):
        ty, th, tc = (y + dy) % NY, (h + dh) % NH, (c + dc) % NC
        tx, tz = (x + dx) % NX, z + dz
        return (ty * 4 + th * 2 + tc, tx * NZ + tz)

    def ring(step):
        at = (h * NZ + z + step + NH * NZ) % (NH * NZ)
        return (y * 4 + (at // NZ) * 2 + c, x * NZ + at % NZ)

    rows, width = act.shape
    slab = NX * rows
    part, half = slab // NY, slab // NY // NH
    queries = query.shape[0]

    mine = pl.ds(pl.multiple_of(x * rows, rows), rows)
    loads = [
        pltpu.make_async_copy(act, ag.at[0, z, mine], load.at[0]),
        pltpu.make_async_copy(cot, ag.at[1, z, mine], load.at[1]),
        pltpu.make_async_copy(gate_w, gw, load.at[2]),
        pltpu.make_async_copy(down_w, dw, load.at[3]),
    ]
    loads += [
        pltpu.make_async_copy(query.at[q], qt.at[q], load.at[4 + q]) for q in range(queries)
    ]
    for item in loads:
        item.start()

    barrier = pltpu.get_barrier_semaphore()

    def greet(device):
        pl.semaphore_signal(barrier, inc=1, device_id=device, device_id_type=MESH)

    greet(dev(dx=1))
    greet(dev(dx=3))
    for near in range(1, max(REACH, 2) + 1):
        greet(ring(near))
        greet(ring(-near))
    greet(dev(dc=1))
    for dy in range(1, NY):
        greet(dev(dy=dy))
    loads[0].wait()
    loads[1].wait()
    pl.semaphore_wait(barrier, 6 + 2 * max(REACH, 2))

    def tell(level, distance):
        for device in (ring(distance), ring(-distance)):
            pl.semaphore_signal(told.at[level], inc=1, device_id=device, device_id_type=MESH)

    def hear(level):
        pl.semaphore_wait(told.at[level], 2)

    def remote(src, dst, send, recv, device):
        return pltpu.make_async_remote_copy(
            src_ref=src, dst_ref=dst, send_sem=send, recv_sem=recv,
            device_id=device, device_id_type=MESH,
        )

    sides = [(s, d) for s in range(NZ) for d in range(2) if s or not d]

    def valid(s, d):
        return z >= s if d == 0 else z + s <= NZ - 1

    def at_z(s, d):
        return jnp.clip(z - s if d == 0 else z + s, 0, NZ - 1)

    def piece(n, zz, xx):
        return ag.at[n, zz, pl.ds(pl.multiple_of(xx * rows, rows), rows)]

    def z_copy(s, d, n):
        start = (s - 1) // REACH * REACH
        block = piece(n, at_z(start, d), x)
        step = (s - start) * (1 - 2 * d)
        return remote(block, block, z_s.at[d, s, n], z_r.at[d, s, n], dev(dz=step))

    def z_going(s, d):
        start = (s - 1) // REACH * REACH
        step = s - start
        if d == 0:
            return (z >= start) & (z + step <= NZ - 1)
        return (z + start <= NZ - 1) & (z >= step)

    def z_send(start, d, n):
        if start % REACH == 0:
            for s in range(min(start + REACH, NZ - 1), start, -1):
                pl.when(z_going(s, d))(lambda s=s: z_copy(s, d, n).start())

    def z_land(s, d, n):
        block = piece(n, at_z(s, d), x)
        return remote(block, block, z_s.at[d, s, n], z_r.at[d, s, n], dev(dz=2 * d - 1))

    def x_copy(s, d, e, n):
        block = piece(n, at_z(s, d), x)
        k = 2 * s + d
        return remote(block, block, x_s.at[e, k, n], x_r.at[e, k, n], dev(dx=1 + 2 * e))

    def x_land(s, d, e, n):
        block = piece(n, at_z(s, d), (x + 3 - 2 * e) % NX)
        k = 2 * s + d
        return remote(block, block, x_s.at[e, k, n], x_r.at[e, k, n], dev(dx=3 - 2 * e))

    def w_copy(s, d, e):
        block = piece(e, at_z(s, d), (x + 3 - 2 * e) % NX)
        k = 2 * s + d
        return remote(block, block, w_s.at[e, k], w_r.at[e, k], dev(dx=1 + 2 * e))

    def w_land(s, d, e):
        block = piece(e, at_z(s, d), (x + 2) % NX)
        k = 2 * s + d
        return remote(block, block, w_s.at[e, k], w_r.at[e, k], dev(dx=3 - 2 * e))

    def ds_of(s):
        return (0,) if s == 0 else (0, 1)

    def step_z(s):
        for d in ds_of(s):
            def body(d=d):
                for n in range(2):
                    if s:
                        z_land(s, d, n).wait_recv()
                        z_send(s, d, n)
                    else:
                        z_send(0, 0, n)
                        z_send(0, 1, n)
                for n in range(2):
                    x_copy(s, d, n, n).start()
                for n in range(2):
                    x_copy(s, d, 1 - n, n).start()
            pl.when(valid(s, d))(body)

    def step_x(s):
        for d in ds_of(s):
            def body(d=d):
                for e in range(2):
                    x_land(s, d, e, e).wait_recv()
                    w_copy(s, d, e).start()
            pl.when(valid(s, d))(body)

    def step_w(s):
        for d in ds_of(s):
            def body(d=d):
                for e in range(2):
                    x_land(s, d, e, 1 - e).wait_recv()
                    w_land(s, d, e).wait_recv()
            pl.when(valid(s, d))(body)

    def drain_gather():
        for s, d in sides:
            if s:
                def line_body(s=s, d=d):
                    for n in range(2):
                        z_copy(s, d, n).wait_send()
                pl.when(z_going(s, d))(line_body)

            def body(s=s, d=d):
                for e in range(2):
                    for n in range(2):
                        x_copy(s, d, e, n).wait_send()
                    w_copy(s, d, e).wait_send()
            pl.when(valid(s, d))(body)

    def turn_queries(first, count):
        def one(q, carry):
            qg[q] = qt[q].T
            return carry

        lax.fori_loop(first, first + count, one, 0)

    def products(zz, store):
        for n, weight in enumerate((gw, dw)):
            store(n, lax.dot_general(
                ag[n, zz], weight[...], (((1,), (1,)), ((), ())), preferred_element_type=F32
            ))

    def slab_of(k, core):
        first, second = nearest(z, 2 * k), nearest(z, 2 * k + 1)
        return jnp.where(core == 0, first, second)

    def c_copy(k):
        return remote(c_out.at[k], c_in.at[k], c_s.at[k], c_r.at[k], dev(dc=1))

    def stage_products(k):
        def to_peer(n, value):
            c_out[k, n] = value.astype(BF16)

        def to_own(n, value):
            acc[k, n] = value

        products(slab_of(k, 1 - c), to_peer)
        c_copy(k).start()
        products(slab_of(k, c), to_own)

    def y_rows(yy):
        return pl.ds(pl.multiple_of(yy * part, part), part)

    def y_copy(k, dy):
        return remote(
            y_out.at[k, :, y_rows((y + dy) % NY)], y_in.at[k, dy - 1],
            y_s.at[k, dy - 1], y_r.at[k, dy - 1], dev(dy=dy),
        )

    def stage_core(k):
        c_copy(k).wait_recv()
        total = acc[k] + c_in[k].astype(F32)
        acc[k] = total
        y_out[k] = total.astype(BF16)
        for dy in (2, 1, 3):
            y_copy(k, dy).start()

    def h_rows(hh):
        return pl.ds(pl.multiple_of(hh * half, half), half)

    def h_copy(k):
        if WHOLE_H[k]:
            return remote(h_out.at[k], h_in.at[k], h_s.at[k], h_r.at[k], dev(dh=1))
        return remote(
            h_out.at[k, :, h_rows(1 - h)], h_in.at[k, :, pl.ds(0, half)],
            h_s.at[k], h_r.at[k], dev(dh=1),
        )

    def stage_y(k):
        total = acc[k, :, y_rows(y)]
        for dy in range(1, NY):
            y_copy(k, dy).wait_recv()
            total = total + y_in[k, dy - 1].astype(F32)
        acc2[k] = total
        h_out[k] = total.astype(BF16)
        h_copy(k).start()

    def s_rows(yy, hh):
        return pl.ds(pl.multiple_of(yy * part + hh * half, half), half)

    def hs_copy(k):
        block = sig.at[k, c, s_rows(y, h)]
        return remote(block, block, hs_s.at[k], hs_r.at[k], dev(dh=1))

    def hs_land(k):
        block = sig.at[k, c, s_rows(y, 1 - h)]
        return remote(block, block, hs_s.at[k], hs_r.at[k], dev(dh=1))

    def ys_copy(k, dy):
        block = sig.at[k, c, y_rows(y)]
        return remote(block, block, ys_s.at[k, dy - 1], ys_r.at[k, dy - 1], dev(dy=dy))

    def ys_land(k, dy):
        block = sig.at[k, c, y_rows((y + NY - dy) % NY)]
        return remote(block, block, ys_s.at[k, dy - 1], ys_r.at[k, dy - 1], dev(dy=dy))

    def cs_copy(k):
        block = sig.at[k, c]
        return remote(block, block, cs_s.at[k], cs_r.at[k], dev(dc=1))

    def cs_land(k):
        block = sig.at[k, 1 - c]
        return remote(block, block, cs_s.at[k], cs_r.at[k], dev(dc=1))

    def signal_of(total):
        gate, back = total[0], total[1]
        return (gate / (1.0 + jnp.exp(-gate)) * back).astype(BF16)

    def stage_h(k):
        h_copy(k).wait_recv()
        if WHOLE_H[k]:
            sig[k, c, y_rows(y)] = signal_of(acc2[k] + h_in[k].astype(F32))
            for dy in (2, 1, 3):
                ys_copy(k, dy).start()
        else:
            total = acc2[k, :, h_rows(h)] + h_in[k, :, pl.ds(0, half)].astype(F32)
            sig[k, c, s_rows(y, h)] = signal_of(total)
            hs_copy(k).start()

    def stage_hs(k):
        if not WHOLE_H[k]:
            hs_land(k).wait_recv()
            for dy in (2, 1, 3):
                ys_copy(k, dy).start()

    def stage_ys(k):
        for dy in range(1, NY):
            ys_land(k, dy).wait_recv()
        cs_copy(k).start()

    def turn(k):
        for n in range(2):
            actt[k, :, n * slab:(n + 1) * slab] = ag[0, nearest(z, 2 * k + n)].astype(F32).T

    def stage_scores(k):
        cs_land(k).wait_recv()
        both = sig[k].reshape(2 * slab, sig.shape[-1])
        first, second = nearest(z, 2 * k), nearest(z, 2 * k + 1)

        def one(q, carry):
            back = lax.dot_general(
                qg[q], both, (((1,), (1,)), ((), ())), preferred_element_type=F32
            )
            line = jnp.sum(back * actt[k], axis=0, keepdims=True)
            scores[first, pl.ds(q, 1), :] = line[:, :slab]
            scores[second, pl.ds(q, 1), :] = line[:, slab:]
            return carry

        lax.fori_loop(0, queries, one, 0, unroll=4)

    def drain_chunk(k):
        c_copy(k).wait_send()
        h_copy(k).wait_send()
        if not WHOLE_H[k]:
            hs_copy(k).wait_send()
        for dy in range(1, NY):
            y_copy(k, dy).wait_send()
            ys_copy(k, dy).wait_send()
        cs_copy(k).wait_send()

    for step in range(NZ + 2):
        if step < NZ:
            step_z(step)
        if 1 <= step < NZ + 1:
            step_x(step - 1)
        if step >= 2:
            step_w(step - 2)
        if step == 0:
            tell(0, 2)
        elif step == 1:
            hear(0)
            tell(1, 4)
        elif step == 4:
            hear(1)
        if step < 4:
            for q in (2 * step, 2 * step + 1):
                loads[4 + q].wait()
            turn_queries(2 * step, 2)
        if step == 2:
            loads[2].wait()
            loads[3].wait()
        ready = step - 2
        if ready >= 1 and ready % 2 == 1:
            k = ready // 2
            stage_products(k)
            turn(k)
        if ready >= 1:
            k = (ready - 1) // 2
            if ready % 2 == 0:
                stage_core(k)
            elif k >= 1:
                stage_y(k - 1)
        if step == 7:
            stage_h(0)
        elif step == 9:
            stage_hs(0)
            stage_h(1)
    last = CHUNKS - 1
    stage_core(last)
    stage_ys(0)
    stage_y(last)
    stage_scores(0)
    stage_h(2)
    stage_hs(1)
    stage_ys(1)
    stage_scores(1)
    stage_h(last)
    stage_hs(2)
    stage_ys(2)
    stage_ys(last)
    stage_scores(2)
    stage_scores(last)

    def by_dest(core):
        return [(hh, xh, 4 * hh + 2 * core + xh) for hh in range(2) for xh in range(2)]

    f1_copies = [
        remote(
            scores.at[pl.ds(pl.multiple_of(4 * hh + 2 * (1 - c), 2), 2)], f1_in.at[hh],
            f1_s.at[hh], f1_r.at[hh], dev(dc=1),
        )
        for hh in range(2)
    ]
    for item in f1_copies:
        item.start()
    for item in f1_copies:
        item.wait_recv()
    for hh, xh, tile in by_dest(c):
        f1_acc[xh, hh] = scores[tile] + f1_in[hh, xh]

    f2_copies = []
    for dx in range(NX):
        for dy in range(NY):
            if dx or dy:
                n = dx * NY + dy - 1
                f2_copies.append(
                    remote(
                        f1_acc.at[((x + dx) % NX) // 2], f2_in.at[n],
                        f2_s.at[n], f2_r.at[n], dev(dx=dx, dy=dy),
                    )
                )
    for item in f2_copies:
        item.start()
    total = f1_acc[x // 2]
    for n, item in enumerate(f2_copies):
        item.wait_recv()
        total = total + f2_in[n]
    f2_acc[...] = total

    f3_copies = []
    for dh in range(NH):
        for dz in range(NZ):
            if dh or dz:
                n = dh * NZ + dz - 1
                tz = (z + dz) % NZ
                f3_copies.append(
                    remote(
                        f2_acc.at[(h + dh) % NH], f3_in.at[n],
                        f3_s.at[n], f3_r.at[n], dev(dh=dh, dz=tz - z),
                    )
                )
    for item in reversed(f3_copies):
        item.start()
    total = f2_acc[h]
    for n, item in enumerate(f3_copies):
        item.wait_recv()
        total = total + f3_in[n]
    lane = y * 32 + (x % 2) * 16 + z * 2
    moved = pltpu.roll(total, (slab - lane) % slab, 1)
    out[...] = moved.T[0:2, :]

    drain_gather()
    for k in range(CHUNKS):
        drain_chunk(k)
    for item in f1_copies + f2_copies + f3_copies:
        item.wait_send()


def per_device(activations, cotangents, gate_weight, down_weight, query_grads):
    rows, width = activations.shape
    hidden = gate_weight.shape[1]
    queries = query_grads.shape[0]
    slab = NX * rows
    part = slab // NY
    dma, vmem = pltpu.SemaphoreType.DMA, pltpu.VMEM
    n = CHUNKS
    scratch = [
        vmem((2, NZ, slab, width), BF16),
        vmem((hidden, width), BF16),
        vmem((hidden, width), BF16),
        vmem((queries, hidden, width), BF16),
        vmem((queries, width, hidden), BF16),
        vmem((n, width, 2 * slab), F32),
        vmem((n, 2, slab, hidden), BF16),
        vmem((n, 2, slab, hidden), BF16),
        vmem((n, 2, slab, hidden), F32),
        vmem((n, 2, slab, hidden), BF16),
        vmem((n, NY - 1, 2, part, hidden), BF16),
        vmem((n, 2, part, hidden), F32),
        vmem((n, 2, part, hidden), BF16),
        vmem((n, 2, part, hidden), BF16),
        vmem((n, 2, slab, hidden), BF16),
        vmem((NZ, queries, slab), F32),
        vmem((2, 2, queries, slab), F32),
        vmem((2, 2, queries, slab), F32),
        vmem((NX * NY - 1, 2, queries, slab), F32),
        vmem((2, queries, slab), F32),
        vmem((NH * NZ - 1, queries, slab), F32),
        pltpu.SemaphoreType.REGULAR((2,)),
        dma((4 + queries,)),
        dma((2, NZ, 2)), dma((2, NZ, 2)),
        dma((2, 2 * NZ, 2)), dma((2, 2 * NZ, 2)),
        dma((2, 2 * NZ)), dma((2, 2 * NZ)),
        dma((n,)), dma((n,)),
        dma((n, NY - 1)), dma((n, NY - 1)),
        dma((n,)), dma((n,)),
        dma((n,)), dma((n,)),
        dma((n, NY - 1)), dma((n, NY - 1)),
        dma((n,)), dma((n,)),
        dma((2,)), dma((2,)),
        dma((NX * NY - 1,)), dma((NX * NY - 1,)),
        dma((NH * NZ - 1,)), dma((NH * NZ - 1,)),
    ]
    return pl.pallas_call(
        kernel,
        name="influence_scores",
        out_shape=jax.ShapeDtypeStruct((2, queries), F32),
        in_specs=[pl.BlockSpec(memory_space=pl.ANY)] * 5,
        out_specs=pl.BlockSpec(memory_space=pltpu.VMEM),
        scratch_shapes=scratch,
        cost_estimate=pl.CostEstimate(
            flops=2 * NZ * slab * width * hidden * (2 + queries),
            bytes_accessed=2 * width * hidden * (2 + queries),
            transcendentals=2 * part * hidden,
        ),
        compiler_params=pltpu.CompilerParams(
            collective_id=0, has_side_effects=True, vmem_limit_bytes=56 * 2**20
        ),
    )(activations, cotangents, gate_weight.T, down_weight, jnp.swapaxes(query_grads, 1, 2))


def solution(mesh):
    placed = (
        P("fsdp", "dp"),
        P("fsdp", "dp"),
        P("dp", "fsdp"),
        P("fsdp", "dp"),
        P(None, "dp", "fsdp"),
    )
    return jax.shard_map(
        per_device, mesh=mesh, in_specs=placed, out_specs=P(("dp", "fsdp"), None), check_vma=False
    )
```

```python
import functools

import jax
import jax.numpy as jnp
from jax import lax
from jax.experimental import pallas as pl
from jax.experimental.pallas import tpu as pltpu
from jax.sharding import PartitionSpec as P

MESH = pl.DeviceIdType.MESH
F32 = jnp.float32
BF16 = jnp.bfloat16
NY, NH, NC, NX, NZ = 4, 2, 2, 4, 8
REACH = 1
CHUNKS = 4
WHOLE_H = (False, False, False, True)


def nearest(z, i):
    reach = jnp.minimum(z, NZ - 1 - z)
    inner = z - (i + 1) // 2 if i % 2 else z + i // 2
    outer = jnp.where(z < NZ // 2, i, NZ - 1 - i)
    return jnp.where(i <= 2 * reach, inner, outer)


def kernel(
    act, cot, gate_w, down_w, query, out,
    ag, gw, dw, qt, qg, actt,
    c_out, c_in, acc, y_out, y_in, acc2, h_out, h_in, sig,
    scores, f1_in, f1_acc, f2_in, f2_acc, f3_in,
    told, load, z_s, z_r, x_s, x_r, w_s, w_r,
    c_s, c_r, y_s, y_r, h_s, h_r, hs_s, hs_r, ys_s, ys_r, cs_s, cs_r,
    f1_s, f1_r, f2_s, f2_r, f3_s, f3_r,
):
    p, f = lax.axis_index("dp"), lax.axis_index("fsdp")
    y, h, c = p // 4, (p // 2) % 2, p % 2
    x, z = f // NZ, f % NZ

    def dev(dy=0, dh=0, dc=0, dx=0, dz=0):
        ty, th, tc = (y + dy) % NY, (h + dh) % NH, (c + dc) % NC
        tx, tz = (x + dx) % NX, z + dz
        return (ty * 4 + th * 2 + tc, tx * NZ + tz)

    def ring(step):
        at = (h * NZ + z + step + NH * NZ) % (NH * NZ)
        return (y * 4 + (at // NZ) * 2 + c, x * NZ + at % NZ)

    rows, width = act.shape
    slab = NX * rows
    part, half = slab // NY, slab // NY // NH
    queries = query.shape[0]

    mine = pl.ds(pl.multiple_of(x * rows, rows), rows)
    loads = [
        pltpu.make_async_copy(act, ag.at[0, z, mine], load.at[0]),
        pltpu.make_async_copy(cot, ag.at[1, z, mine], load.at[1]),
        pltpu.make_async_copy(gate_w, gw, load.at[2]),
        pltpu.make_async_copy(down_w, dw, load.at[3]),
    ]
    loads += [
        pltpu.make_async_copy(query.at[q], qt.at[q], load.at[4 + q]) for q in range(queries)
    ]
    for item in loads:
        item.start()

    barrier = pltpu.get_barrier_semaphore()

    def greet(device):
        pl.semaphore_signal(barrier, inc=1, device_id=device, device_id_type=MESH)

    greet(dev(dx=1))
    greet(dev(dx=3))
    for near in range(1, max(REACH, 2) + 1):
        greet(ring(near))
        greet(ring(-near))
    greet(dev(dc=1))
    for dy in range(1, NY):
        greet(dev(dy=dy))
    loads[0].wait()
    loads[1].wait()
    pl.semaphore_wait(barrier, 6 + 2 * max(REACH, 2))

    def tell(level, distance):
        for device in (ring(distance), ring(-distance)):
            pl.semaphore_signal(told.at[level], inc=1, device_id=device, device_id_type=MESH)

    def hear(level):
        pl.semaphore_wait(told.at[level], 2)

    def remote(src, dst, send, recv, device):
        return pltpu.make_async_remote_copy(
            src_ref=src, dst_ref=dst, send_sem=send, recv_sem=recv,
            device_id=device, device_id_type=MESH,
        )

    sides = [(s, d) for s in range(NZ) for d in range(2) if s or not d]

    def valid(s, d):
        return z >= s if d == 0 else z + s <= NZ - 1

    def at_z(s, d):
        return jnp.clip(z - s if d == 0 else z + s, 0, NZ - 1)

    def piece(n, zz, xx):
        return ag.at[n, zz, pl.ds(pl.multiple_of(xx * rows, rows), rows)]

    def both(zz, xx):
        return ag.at[:, zz, pl.ds(pl.multiple_of(xx * rows, rows), rows)]

    def z_copy(s, d, n):
        start = (s - 1) // REACH * REACH
        block = both(at_z(start, d), x)
        step = (s - start) * (1 - 2 * d)
        return remote(block, block, z_s.at[d, s, 0], z_r.at[d, s, 0], dev(dz=step))

    def z_going(s, d):
        start = (s - 1) // REACH * REACH
        step = s - start
        if d == 0:
            return (z >= start) & (z + step <= NZ - 1)
        return (z + start <= NZ - 1) & (z >= step)

    def z_send(start, d, n):
        if start % REACH == 0:
            for s in range(min(start + REACH, NZ - 1), start, -1):
                pl.when(z_going(s, d))(lambda s=s: z_copy(s, d, n).start())

    def z_land(s, d, n):
        block = both(at_z(s, d), x)
        return remote(block, block, z_s.at[d, s, 0], z_r.at[d, s, 0], dev(dz=2 * d - 1))

    def x_copy(s, d, e, n):
        block = piece(n, at_z(s, d), x)
        k = 2 * s + d
        return remote(block, block, x_s.at[e, k, n], x_r.at[e, k, n], dev(dx=1 + 2 * e))

    def x_land(s, d, e, n):
        block = piece(n, at_z(s, d), (x + 3 - 2 * e) % NX)
        k = 2 * s + d
        return remote(block, block, x_s.at[e, k, n], x_r.at[e, k, n], dev(dx=3 - 2 * e))

    def w_copy(s, d, e):
        block = piece(e, at_z(s, d), (x + 3 - 2 * e) % NX)
        k = 2 * s + d
        return remote(block, block, w_s.at[e, k], w_r.at[e, k], dev(dx=1 + 2 * e))

    def w_land(s, d, e):
        block = piece(e, at_z(s, d), (x + 2) % NX)
        k = 2 * s + d
        return remote(block, block, w_s.at[e, k], w_r.at[e, k], dev(dx=3 - 2 * e))

    def ds_of(s):
        return (0,) if s == 0 else (0, 1)

    def step_z(s):
        for d in ds_of(s):
            def body(d=d):
                if s:
                    z_land(s, d, 0).wait_recv()
                    z_send(s, d, 0)
                else:
                    z_send(0, 0, 0)
                    z_send(0, 1, 0)
                for n in range(2):
                    x_copy(s, d, n, n).start()
                for n in range(2):
                    x_copy(s, d, 1 - n, n).start()
            pl.when(valid(s, d))(body)

    def step_x(s):
        for d in ds_of(s):
            def body(d=d):
                for e in range(2):
                    x_land(s, d, e, e).wait_recv()
                    w_copy(s, d, e).start()
            pl.when(valid(s, d))(body)

    def step_w(s):
        for d in ds_of(s):
            def body(d=d):
                for e in range(2):
                    x_land(s, d, e, 1 - e).wait_recv()
                    w_land(s, d, e).wait_recv()
            pl.when(valid(s, d))(body)

    def drain_gather():
        for s, d in sides:
            if s:
                def line_body(s=s, d=d):
                    z_copy(s, d, 0).wait_send()
                pl.when(z_going(s, d))(line_body)

            def body(s=s, d=d):
                for e in range(2):
                    for n in range(2):
                        x_copy(s, d, e, n).wait_send()
                    w_copy(s, d, e).wait_send()
            pl.when(valid(s, d))(body)

    def turn_queries(first, count):
        def one(q, carry):
            qg[q] = qt[q].T
            return carry

        lax.fori_loop(first, first + count, one, 0)

    def products(zz, store):
        for n, weight in enumerate((gw, dw)):
            store(n, lax.dot_general(
                ag[n, zz], weight[...], (((1,), (1,)), ((), ())), preferred_element_type=F32
            ))

    def slab_of(k, core):
        first, second = nearest(z, 2 * k), nearest(z, 2 * k + 1)
        return jnp.where(core == 0, first, second)

    def c_copy(k):
        return remote(c_out.at[k], c_in.at[k], c_s.at[k], c_r.at[k], dev(dc=1))

    def stage_products(k):
        def to_peer(n, value):
            c_out[k, n] = value.astype(BF16)

        def to_own(n, value):
            acc[k, n] = value

        products(slab_of(k, 1 - c), to_peer)
        c_copy(k).start()
        products(slab_of(k, c), to_own)

    def y_rows(yy):
        return pl.ds(pl.multiple_of(yy * part, part), part)

    def y_copy(k, dy):
        return remote(
            y_out.at[k, :, y_rows((y + dy) % NY)], y_in.at[k, dy - 1],
            y_s.at[k, dy - 1], y_r.at[k, dy - 1], dev(dy=dy),
        )

    def stage_core(k):
        c_copy(k).wait_recv()
        total = acc[k] + c_in[k].astype(F32)
        acc[k] = total
        y_out[k] = total.astype(BF16)
        for dy in (2, 1, 3):
            y_copy(k, dy).start()

    def h_rows(hh):
        return pl.ds(pl.multiple_of(hh * half, half), half)

    def h_copy(k):
        if WHOLE_H[k]:
            return remote(h_out.at[k], h_in.at[k], h_s.at[k], h_r.at[k], dev(dh=1))
        return remote(
            h_out.at[k, :, h_rows(1 - h)], h_in.at[k, :, pl.ds(0, half)],
            h_s.at[k], h_r.at[k], dev(dh=1),
        )

    def stage_y(k):
        total = acc[k, :, y_rows(y)]
        for dy in range(1, NY):
            y_copy(k, dy).wait_recv()
            total = total + y_in[k, dy - 1].astype(F32)
        acc2[k] = total
        h_out[k] = total.astype(BF16)
        h_copy(k).start()

    def s_rows(yy, hh):
        return pl.ds(pl.multiple_of(yy * part + hh * half, half), half)

    def hs_copy(k):
        block = sig.at[k, c, s_rows(y, h)]
        return remote(block, block, hs_s.at[k], hs_r.at[k], dev(dh=1))

    def hs_land(k):
        block = sig.at[k, c, s_rows(y, 1 - h)]
        return remote(block, block, hs_s.at[k], hs_r.at[k], dev(dh=1))

    def ys_copy(k, dy):
        block = sig.at[k, c, y_rows(y)]
        return remote(block, block, ys_s.at[k, dy - 1], ys_r.at[k, dy - 1], dev(dy=dy))

    def ys_land(k, dy):
        block = sig.at[k, c, y_rows((y + NY - dy) % NY)]
        return remote(block, block, ys_s.at[k, dy - 1], ys_r.at[k, dy - 1], dev(dy=dy))

    def cs_copy(k):
        block = sig.at[k, c]
        return remote(block, block, cs_s.at[k], cs_r.at[k], dev(dc=1))

    def cs_land(k):
        block = sig.at[k, 1 - c]
        return remote(block, block, cs_s.at[k], cs_r.at[k], dev(dc=1))

    def signal_of(total):
        gate, back = total[0], total[1]
        return (gate / (1.0 + jnp.exp(-gate)) * back).astype(BF16)

    def stage_h(k):
        h_copy(k).wait_recv()
        if WHOLE_H[k]:
            sig[k, c, y_rows(y)] = signal_of(acc2[k] + h_in[k].astype(F32))
            for dy in (2, 1, 3):
                ys_copy(k, dy).start()
        else:
            total = acc2[k, :, h_rows(h)] + h_in[k, :, pl.ds(0, half)].astype(F32)
            sig[k, c, s_rows(y, h)] = signal_of(total)
            hs_copy(k).start()

    def stage_hs(k):
        if not WHOLE_H[k]:
            hs_land(k).wait_recv()
            for dy in (2, 1, 3):
                ys_copy(k, dy).start()

    def stage_ys(k):
        for dy in range(1, NY):
            ys_land(k, dy).wait_recv()
        cs_copy(k).start()

    def turn(k):
        for n in range(2):
            actt[k, :, n * slab:(n + 1) * slab] = ag[0, nearest(z, 2 * k + n)].astype(F32).T

    def stage_scores(k):
        cs_land(k).wait_recv()
        both = sig[k].reshape(2 * slab, sig.shape[-1])
        first, second = nearest(z, 2 * k), nearest(z, 2 * k + 1)

        def one(q, carry):
            back = lax.dot_general(
                qg[q], both, (((1,), (1,)), ((), ())), preferred_element_type=F32
            )
            line = jnp.sum(back * actt[k], axis=0, keepdims=True)
            scores[first, pl.ds(q, 1), :] = line[:, :slab]
            scores[second, pl.ds(q, 1), :] = line[:, slab:]
            return carry

        lax.fori_loop(0, queries, one, 0, unroll=4)

    def drain_chunk(k):
        c_copy(k).wait_send()
        h_copy(k).wait_send()
        if not WHOLE_H[k]:
            hs_copy(k).wait_send()
        for dy in range(1, NY):
            y_copy(k, dy).wait_send()
            ys_copy(k, dy).wait_send()
        cs_copy(k).wait_send()

    for step in range(NZ + 2):
        if step < NZ:
            step_z(step)
        if 1 <= step < NZ + 1:
            step_x(step - 1)
        if step >= 2:
            step_w(step - 2)
        if step == 0:
            tell(0, 2)
        elif step == 1:
            hear(0)
            tell(1, 4)
        elif step == 4:
            hear(1)
        if step < 4:
            for q in (2 * step, 2 * step + 1):
                loads[4 + q].wait()
            turn_queries(2 * step, 2)
        if step == 2:
            loads[2].wait()
            loads[3].wait()
        ready = step - 2
        if ready >= 1 and ready % 2 == 1:
            k = ready // 2
            stage_products(k)
            turn(k)
        if ready >= 1:
            k = (ready - 1) // 2
            if ready % 2 == 0:
                stage_core(k)
            elif k >= 1:
                stage_y(k - 1)
        if step == 7:
            stage_h(0)
        elif step == 9:
            stage_hs(0)
            stage_h(1)
    last = CHUNKS - 1
    stage_core(last)
    stage_ys(0)
    stage_y(last)
    stage_scores(0)
    stage_h(2)
    stage_hs(1)
    stage_h(last)
    stage_hs(2)
    stage_ys(1)
    stage_scores(1)
    stage_ys(2)
    stage_ys(last)
    stage_scores(2)
    stage_scores(last)

    def by_dest(core):
        return [(hh, xh, 4 * hh + 2 * core + xh) for hh in range(2) for xh in range(2)]

    f1_copies = [
        remote(
            scores.at[pl.ds(pl.multiple_of(4 * hh + 2 * (1 - c), 2), 2)], f1_in.at[hh],
            f1_s.at[hh], f1_r.at[hh], dev(dc=1),
        )
        for hh in range(2)
    ]
    for item in f1_copies:
        item.start()
    for item in f1_copies:
        item.wait_recv()
    for hh, xh, tile in by_dest(c):
        f1_acc[xh, hh] = scores[tile] + f1_in[hh, xh]

    f2_copies = []
    for dx in range(NX):
        for dy in range(NY):
            if dx or dy:
                n = dx * NY + dy - 1
                f2_copies.append(
                    remote(
                        f1_acc.at[((x + dx) % NX) // 2], f2_in.at[n],
                        f2_s.at[n], f2_r.at[n], dev(dx=dx, dy=dy),
                    )
                )
    for dx, dy in sorted(
        ((dx, dy) for dx in range(NX) for dy in range(NY) if dx or dy),
        key=lambda to: -min(to[0], NX - to[0]) - min(to[1], NY - to[1]),
    ):
        f2_copies[dx * NY + dy - 1].start()
    total = f1_acc[x // 2]
    for n, item in enumerate(f2_copies):
        item.wait_recv()
        total = total + f2_in[n]
    f2_acc[...] = total

    f3_copies = []
    for dh in range(NH):
        for dz in range(NZ):
            if dh or dz:
                n = dh * NZ + dz - 1
                tz = (z + dz) % NZ
                f3_copies.append(
                    remote(
                        f2_acc.at[(h + dh) % NH], f3_in.at[n],
                        f3_s.at[n], f3_r.at[n], dev(dh=dh, dz=tz - z),
                    )
                )
    for n in (*range(NZ - 1, NH * NZ - 1), *range(NZ - 2, -1, -1)):
        f3_copies[n].start()
    total = f2_acc[h]
    for n, item in enumerate(f3_copies):
        item.wait_recv()
        total = total + f3_in[n]
    lane = y * 32 + (x % 2) * 16 + z * 2
    moved = pltpu.roll(total, (slab - lane) % slab, 1)
    out[...] = moved.T[0:2, :]

    drain_gather()
    for k in range(CHUNKS):
        drain_chunk(k)
    for item in f1_copies + f2_copies + f3_copies:
        item.wait_send()


def per_device(activations, cotangents, gate_weight, down_weight, query_grads):
    rows, width = activations.shape
    hidden = gate_weight.shape[1]
    queries = query_grads.shape[0]
    slab = NX * rows
    part = slab // NY
    dma, vmem = pltpu.SemaphoreType.DMA, pltpu.VMEM
    n = CHUNKS
    scratch = [
        vmem((2, NZ, slab, width), BF16),
        vmem((hidden, width), BF16),
        vmem((hidden, width), BF16),
        vmem((queries, hidden, width), BF16),
        vmem((queries, width, hidden), BF16),
        vmem((n, width, 2 * slab), F32),
        vmem((n, 2, slab, hidden), BF16),
        vmem((n, 2, slab, hidden), BF16),
        vmem((n, 2, slab, hidden), F32),
        vmem((n, 2, slab, hidden), BF16),
        vmem((n, NY - 1, 2, part, hidden), BF16),
        vmem((n, 2, part, hidden), F32),
        vmem((n, 2, part, hidden), BF16),
        vmem((n, 2, part, hidden), BF16),
        vmem((n, 2, slab, hidden), BF16),
        vmem((NZ, queries, slab), F32),
        vmem((2, 2, queries, slab), F32),
        vmem((2, 2, queries, slab), F32),
        vmem((NX * NY - 1, 2, queries, slab), F32),
        vmem((2, queries, slab), F32),
        vmem((NH * NZ - 1, queries, slab), F32),
        pltpu.SemaphoreType.REGULAR((2,)),
        dma((4 + queries,)),
        dma((2, NZ, 2)), dma((2, NZ, 2)),
        dma((2, 2 * NZ, 2)), dma((2, 2 * NZ, 2)),
        dma((2, 2 * NZ)), dma((2, 2 * NZ)),
        dma((n,)), dma((n,)),
        dma((n, NY - 1)), dma((n, NY - 1)),
        dma((n,)), dma((n,)),
        dma((n,)), dma((n,)),
        dma((n, NY - 1)), dma((n, NY - 1)),
        dma((n,)), dma((n,)),
        dma((2,)), dma((2,)),
        dma((NX * NY - 1,)), dma((NX * NY - 1,)),
        dma((NH * NZ - 1,)), dma((NH * NZ - 1,)),
    ]
    return pl.pallas_call(
        kernel,
        name="influence_scores",
        out_shape=jax.ShapeDtypeStruct((2, queries), F32),
        in_specs=[pl.BlockSpec(memory_space=pl.ANY)] * 5,
        out_specs=pl.BlockSpec(memory_space=pltpu.VMEM),
        scratch_shapes=scratch,
        cost_estimate=pl.CostEstimate(
            flops=2 * NZ * slab * width * hidden * (2 + queries),
            bytes_accessed=2 * width * hidden * (2 + queries),
            transcendentals=2 * part * hidden,
        ),
        compiler_params=pltpu.CompilerParams(
            collective_id=0, has_side_effects=True, vmem_limit_bytes=56 * 2**20
        ),
    )(activations, cotangents, gate_weight.T, down_weight, jnp.swapaxes(query_grads, 1, 2))


def solution(mesh):
    placed = (
        P("fsdp", "dp"),
        P("fsdp", "dp"),
        P("dp", "fsdp"),
        P("fsdp", "dp"),
        P(None, "dp", "fsdp"),
    )
    return jax.shard_map(
        per_device, mesh=mesh, in_specs=placed, out_specs=P(("dp", "fsdp"), None), check_vma=False
    )
```
